512 devices in a mesh: bfly: 32 (over y, x), sec: 2 (over core), probe: 8 (over z).
Axes of the slice: x: 4, y: 8, z: 8, core: 2. Of those that a mesh axis runs over, the one named last changes fastest.
Arguments:
- probes: bfloat16 [512, 1024, 256], P('bfly', 'probe'), may hold values from -6 to 6
- mixers: bfloat16 [9, 2, 256, 256], replicated, may hold values from -0.25 to 0.25
- box_gains: float32 [4, 512, 256], P(None, 'bfly'), may hold values from 0.1 to 1.9
- box_orders: int32 [4, 512], P(None, 'bfly'), may hold values from 0 to 15, as said below
- near_count: int32 [512], P('bfly'), may hold values from 1 to 6, as said below
- near_cols: int32 [512, 6], P('bfly'), may hold values from 0 to 511, as said below
- near_scale: float32 [512, 6, 256], P('bfly'), may hold values from 0.1 to 1.9
- near_table: bfloat16 [6, 256, 256], P(None, 'probe'), may hold values from -0.1875 to 0.1875
Outputs:
- response: float32 [512, 1024, 256], P('bfly', 'probe')
The draws below stay inside these ranges and needn't reach their ends.
Inputs may be any that keep to these rules, and one draw needn't show every extreme that they name: `box_orders`: each aligned block of 16 entries of a row is a permutation of 0 to 15. `near_count`: some box row has 6 blocks. `near_cols`: each block's box lies within 8 boxes of its row's box.
All inputs are finite; a program needn't handle non-finite values.
Results may differ from the reference program's by a relative error of at most 0.02.
Values may be sent and summed in bfloat16 or wider, within the bound.
No kernel may reach another device: no remote copies, remote signals or barrier semaphores. Data moves between devices by JAX's collectives and lax.ppermute only.
A program may use at most 64 MiB of HBM per device.

```python
import jax
import jax.numpy as jnp
from jax import lax

W = 256
BOX_DEV = 16
LOCAL = 4
MAXB = 6
CROSS = 5
LEVELS = 9
NBOX = 512
PROBES = 1024
RIM = 8
N_BFLY = 32


def draw_box_orders(key, part):
    key = jax.random.fold_in(key, 13)
    key_list = jax.random.split(key, LOCAL * N_BFLY)

    def shuffle(single_key):
        return jax.random.permutation(single_key, BOX_DEV)
    shuffled = jax.vmap(shuffle)(key_list)
    return shuffled.reshape(LOCAL, NBOX).astype(jnp.int32)


def draw_near_count(key, part):
    key = jax.random.fold_in(key, 11)
    cap_key, busy_key, row_key = jax.random.split(key, 3)
    ceilings = jax.random.randint(cap_key, (N_BFLY,), 1, MAXB + 1)
    busiest = jax.random.randint(busy_key, (), 0, N_BFLY)
    ceilings = jnp.where(jnp.arange(N_BFLY) == busiest, MAXB, ceilings)
    counts = jax.random.randint(row_key, (N_BFLY, BOX_DEV), 1, ceilings[:, None] + 1)
    counts = counts.at[:, 0].set(ceilings)
    return counts.reshape(NBOX).astype(jnp.int32)


def draw_near_cols(key, part):
    key = jax.random.fold_in(key, 12)
    offsets = jax.random.randint(key, (NBOX, MAXB), -RIM, RIM + 1)
    centres = jnp.arange(NBOX)[:, None]
    columns = jnp.clip(centres + offsets, 0, NBOX - 1)
    columns = columns.at[0, 0].set(0).at[NBOX - 1, 0].set(NBOX - 1)
    return columns.astype(jnp.int32)


def shard_levels(rng, extent, cuts, smallest, largest):
    level, own = 1.0, jax.random.fold_in(rng, 6)
    for axis_at, blocks in cuts:
        steps = jnp.exp(jax.random.uniform(jax.random.fold_in(own, axis_at), (blocks,), jnp.float32, smallest / len(cuts), largest / len(cuts)))
        level = level * jnp.repeat(steps, extent[axis_at] // blocks).reshape([-1 if axis == axis_at else 1 for axis in range(len(extent))])
    return level


def normal_values(own_key, shape, width, most, pieces=(), held_as=jnp.bfloat16):
    loudness = shard_levels(own_key, shape, pieces, -0.22, 0.18) if pieces else 1.0
    result = jax.random.normal(own_key, shape, jnp.float32) * width * loudness
    return jnp.minimum(jnp.maximum(result, -most), most).astype(held_as)


def setup_inputs(seed: int = 0) -> dict:
    key_of = jax.random.split(jax.random.key(seed), 9)
    return {
        "probes": normal_values(key_of[0], (NBOX, PROBES, W), 1.0, 6.0, ((0, 32), (1, 8))),
        "mixers": normal_values(key_of[1], (LEVELS, 2, W, W), (2 * W) ** -0.5, 0.25),
        "box_gains": jnp.clip(1.0 + 0.18 * jax.random.normal(key_of[2], (LOCAL, NBOX, W), jnp.float32), 0.1, 1.9),
        "box_orders": draw_box_orders(jax.random.fold_in(key_of[8], 71), 0),
        "near_count": draw_near_count(jax.random.fold_in(key_of[8], 71), 0),
        "near_cols": draw_near_cols(jax.random.fold_in(key_of[8], 71), 0),
        "near_scale": jnp.clip(1.0 + 0.18 * jax.random.normal(key_of[6], (NBOX, MAXB, W), jnp.float32), 0.1, 1.9),
        "near_table": normal_values(key_of[7], (MAXB, W, W), (4 * W) ** -0.5, 0.1875, ((1, 8),)),
    }


def pair_level(current, stride, weights):
    full_shape = current.shape
    grouped = current.reshape(full_shape[0] // (2 * stride), 2, stride, full_shape[1], full_shape[2])
    partner = grouped[:, ::-1].reshape(full_shape)
    own_rows = current.reshape(-1, full_shape[2])
    other_rows = partner.reshape(-1, full_shape[2])
    product = jnp.dot(own_rows, weights[0], preferred_element_type=jnp.float32)
    product = product + jnp.dot(other_rows, weights[1], preferred_element_type=jnp.float32)
    return product.reshape(full_shape)


def reference(probes, mixers, box_gains, box_orders, near_count, near_cols, near_scale, near_table):
    current = probes
    for level_index in range(LOCAL):
        blocks = current.reshape(N_BFLY, BOX_DEV, PROBES, W)
        ordering = box_orders[level_index].reshape(N_BFLY, BOX_DEV)
        blocks = jax.vmap(lambda block_rows, block_order: jnp.take(block_rows, block_order, axis=0))(blocks, ordering)
        current = blocks.reshape(NBOX, PROBES, W)
        mixed = pair_level(current, 2 ** level_index, mixers[level_index])
        current = (mixed * box_gains[level_index][:, None, :]).astype(jnp.bfloat16)
    for cross_index in range(CROSS):
        current = pair_level(current, BOX_DEV * 2 ** cross_index, mixers[LOCAL + cross_index]).astype(jnp.bfloat16)
    far_term = current.astype(jnp.float32)

    def near_group(group_index):
        row_ids = group_index * 16 + jnp.arange(16, dtype=jnp.int32)
        col_ids = near_cols[row_ids].reshape(-1)
        gathered = probes[col_ids].reshape(16, MAXB, PROBES, W)
        active = jnp.arange(MAXB, dtype=jnp.int32)[None, :] < near_count[row_ids][:, None]
        scaling = near_scale[row_ids] * active[:, :, None].astype(jnp.float32)
        operand = (gathered.astype(jnp.float32) * scaling[:, :, None, :]).astype(jnp.bfloat16)
        return jnp.einsum("bkpw,kwv->bpv", operand.astype(jnp.float32), near_table.astype(jnp.float32))

    near_term = lax.map(near_group, jnp.arange(NBOX // 16, dtype=jnp.int32)).reshape(NBOX, PROBES, W)
    return far_term + near_term
```

```python
import functools

import jax
import jax.numpy as jnp
from jax import lax
from jax.experimental import pallas as pl
from jax.experimental.pallas import tpu as pltpu
from jax.sharding import PartitionSpec as P

LOCAL = 4
MAXB = 6
RIM = 8
VMEM_LIMIT = 40 * 1024 * 1024


def vmem():
    return pl.BlockSpec(memory_space=pltpu.VMEM)


def smem():
    return pl.BlockSpec(memory_space=pltpu.SMEM)


def local_kernel(orders, half, weights, gains, out, pairs):
    boxes, cols, width = half.shape
    for level in range(LOCAL):
        source = half if level == 0 else out
        for box in range(boxes):
            block = source[orders[level, box]]
            pairs[box, :, :width] = block
            pairs[box ^ (1 << level), :, width:] = block
        mixed = jnp.dot(
            pairs[...].reshape(boxes * cols, 2 * width),
            weights[level],
            preferred_element_type=jnp.float32,
        ).reshape(boxes, cols, width)
        out[...] = (mixed * gains[level][:, None, :]).astype(out.dtype)


def cross_kernel(levels, rows, weights, out, pairs):
    count, depth, width = rows.shape
    for level in range(levels):
        source = rows if level == 0 else out
        for box in range(count):
            block = source[box]
            pairs[box, :, :width] = block
            pairs[box ^ (1 << level), :, width:] = block
        out[...] = (
            jnp.dot(
                pairs[...].reshape(count * depth, 2 * width),
                weights[level],
                preferred_element_type=jnp.float32,
            )
            .reshape(count, depth, width)
            .astype(out.dtype)
        )


def near_kernel(base, cols_ref, counts, low, own, high, scale, table, out, extended, operand):
    boxes, cols, width = own.shape
    extended[:RIM] = low[...]
    extended[RIM : RIM + boxes] = own[...]
    extended[RIM + boxes :] = high[...]
    first = base[0] - RIM
    for box in range(boxes):
        for slot in range(MAXB):
            block = extended[cols_ref[box, slot] - first].astype(jnp.float32)
            active = (slot < counts[box]).astype(jnp.float32)
            scaled = block * (scale[box, slot : slot + 1, :] * active)
            operand[box, :, slot * width : (slot + 1) * width] = scaled.astype(operand.dtype)
    out[...] = jnp.dot(
        operand[...].reshape(boxes * cols, MAXB * width),
        table[...],
        preferred_element_type=jnp.float32,
    ).reshape(boxes, cols, width)


def params():
    return pltpu.CompilerParams(vmem_limit_bytes=VMEM_LIMIT)


def cost(rows, depth, width, extra):
    return pl.CostEstimate(
        flops=2 * rows * depth * width, bytes_accessed=extra, transcendentals=0
    )


def shards(probes, mixers, box_gains, box_orders, near_count, near_cols, near_scale, near_table):
    boxes, columns, width = probes.shape
    peers = lax.axis_size("bfly")
    levels = mixers.shape[0] - LOCAL
    sec = lax.axis_index("sec")
    me = lax.axis_index("bfly")
    cols = columns // 2
    rows = boxes * cols
    depth = rows // peers
    stacked = mixers.reshape(mixers.shape[0], 2 * width, width)
    half = lax.dynamic_slice_in_dim(probes, sec * cols, cols, axis=1)

    current = pl.pallas_call(
        local_kernel,
        out_shape=jax.ShapeDtypeStruct((boxes, cols, width), jnp.bfloat16),
        in_specs=[smem(), vmem(), vmem(), vmem()],
        out_specs=vmem(),
        scratch_shapes=[pltpu.VMEM((boxes, cols, 2 * width), jnp.bfloat16)],
        compiler_params=params(),
        cost_estimate=cost(LOCAL * rows, 2 * width, width, 4 * rows * width),
        name="local_levels",
    )(box_orders, half, stacked[:LOCAL], box_gains)

    spread = lax.all_to_all(current.reshape(peers, depth, width), "bfly", 0, 0, tiled=True)

    crossed = pl.pallas_call(
        functools.partial(cross_kernel, levels),
        out_shape=jax.ShapeDtypeStruct((peers, depth, width), jnp.bfloat16),
        in_specs=[vmem(), vmem()],
        out_specs=vmem(),
        scratch_shapes=[pltpu.VMEM((peers, depth, 2 * width), jnp.bfloat16)],
        compiler_params=params(),
        cost_estimate=cost(levels * rows, 2 * width, width, 4 * rows * width),
        name="cross_levels",
    )(spread, stacked[LOCAL:])

    far = lax.all_to_all(crossed, "bfly", 0, 0, tiled=True).reshape(boxes, cols, width)

    up = [(i, i + 1) for i in range(peers - 1)]
    down = [(i + 1, i) for i in range(peers - 1)]
    low = lax.ppermute(half[boxes - RIM :], "bfly", up)
    high = lax.ppermute(half[:RIM], "bfly", down)
    table = lax.all_gather(near_table, "probe", axis=1, tiled=True)

    near = pl.pallas_call(
        near_kernel,
        out_shape=jax.ShapeDtypeStruct((boxes, cols, width), jnp.float32),
        in_specs=[smem(), smem(), smem()] + [vmem()] * 5,
        out_specs=vmem(),
        scratch_shapes=[
            pltpu.VMEM((boxes + 2 * RIM, cols, width), jnp.bfloat16),
            pltpu.VMEM((boxes, cols, MAXB * width), jnp.bfloat16),
        ],
        compiler_params=params(),
        cost_estimate=cost(rows, MAXB * width, width, 8 * rows * width),
        name="near_field",
    )(
        (me * boxes)[None],
        near_cols,
        near_count,
        low,
        half,
        high,
        near_scale,
        table.reshape(MAXB * width, width),
    )

    mine = (far.astype(jnp.float32) + near).astype(jnp.bfloat16)
    other = lax.ppermute(mine, "sec", [(0, 1), (1, 0)])
    first = jnp.where(sec == 0, mine, other)
    second = jnp.where(sec == 0, other, mine)
    return jnp.concatenate([first, second], axis=1).astype(jnp.float32)


def solution(mesh):
    return jax.shard_map(
        shards,
        mesh=mesh,
        in_specs=(
            P("bfly", "probe", None),
            P(),
            P(None, "bfly", None),
            P(None, "bfly"),
            P("bfly"),
            P("bfly", None),
            P("bfly", None, None),
            P(None, "probe", None),
        ),
        out_specs=P("bfly", "probe", None),
        check_vma=False,
    )
```

```python
import functools

import jax
import jax.numpy as jnp
from jax import lax
from jax.experimental import pallas as pl
from jax.experimental.pallas import tpu as pltpu
from jax.sharding import PartitionSpec as P

LOCAL = 4
MAXB = 6
RIM = 8
VMEM_LIMIT = 40 * 1024 * 1024


def vmem():
    return pl.BlockSpec(memory_space=pltpu.VMEM)


def smem():
    return pl.BlockSpec(memory_space=pltpu.SMEM)


def local_kernel(orders, half, weights, gains, out, pairs):
    boxes, cols, width = half.shape
    for level in range(LOCAL):
        source = half if level == 0 else out
        for box in range(boxes):
            block = source[orders[level, box]]
            pairs[box, :, :width] = block
            pairs[box ^ (1 << level), :, width:] = block
        mixed = jnp.dot(
            pairs[...].reshape(boxes * cols, 2 * width),
            weights[level],
            preferred_element_type=jnp.float32,
        ).reshape(boxes, cols, width)
        out[...] = (mixed * gains[level][:, None, :]).astype(out.dtype)


def cross_kernel(levels, rows, weights, out, pairs):
    count, depth, width = rows.shape
    for level in range(levels):
        source = rows if level == 0 else out
        for box in range(count):
            block = source[box]
            pairs[box, :, :width] = block
            pairs[box ^ (1 << level), :, width:] = block
        out[...] = (
            jnp.dot(
                pairs[...].reshape(count * depth, 2 * width),
                weights[level],
                preferred_element_type=jnp.float32,
            )
            .reshape(count, depth, width)
            .astype(out.dtype)
        )


def near_kernel(base, cols_ref, counts, low, own, high, scale, table, out, extended, operand):
    boxes, cols, width = own.shape
    extended[:RIM] = low[...]
    extended[RIM : RIM + boxes] = own[...]
    extended[RIM + boxes :] = high[...]
    first = base[0] - RIM
    for box in range(boxes):
        for slot in range(MAXB):
            block = extended[cols_ref[box, slot] - first].astype(jnp.float32)
            active = (slot < counts[box]).astype(jnp.float32)
            scaled = block * (scale[box, slot : slot + 1, :] * active)
            operand[box, :, slot * width : (slot + 1) * width] = scaled.astype(operand.dtype)
    out[...] = jnp.dot(
        operand[...].reshape(boxes * cols, MAXB * width),
        table[: MAXB * width],
        preferred_element_type=jnp.float32,
    ).reshape(boxes, cols, width)


def params():
    return pltpu.CompilerParams(vmem_limit_bytes=VMEM_LIMIT)


def cost(rows, depth, width, extra):
    return pl.CostEstimate(
        flops=2 * rows * depth * width, bytes_accessed=extra, transcendentals=0
    )


def shards(probes, mixers, box_gains, box_orders, near_count, near_cols, near_scale, near_table):
    boxes, columns, width = probes.shape
    peers = lax.axis_size("bfly")
    levels = mixers.shape[0] - LOCAL
    sec = lax.axis_index("sec")
    me = lax.axis_index("bfly")
    cols = columns // 2
    rows = boxes * cols
    depth = rows // peers
    stacked = mixers.reshape(mixers.shape[0], 2 * width, width)
    half = lax.dynamic_slice_in_dim(probes, sec * cols, cols, axis=1)
    padded = jnp.concatenate([near_table, near_table[:2]], axis=0)
    table = lax.all_gather(padded, "probe", axis=1, tiled=True)

    current = pl.pallas_call(
        local_kernel,
        out_shape=jax.ShapeDtypeStruct((boxes, cols, width), jnp.bfloat16),
        in_specs=[smem(), vmem(), vmem(), vmem()],
        out_specs=vmem(),
        scratch_shapes=[pltpu.VMEM((boxes, cols, 2 * width), jnp.bfloat16)],
        compiler_params=params(),
        cost_estimate=cost(LOCAL * rows, 2 * width, width, 4 * rows * width),
        name="local_levels",
    )(box_orders, half, stacked[:LOCAL], box_gains)

    spread = lax.all_to_all(current.reshape(peers, depth, width), "bfly", 0, 0, tiled=True)

    up = [(i, i + 1) for i in range(peers - 1)]
    down = [(i + 1, i) for i in range(peers - 1)]
    low = lax.ppermute(half[boxes - RIM :], "bfly", up)
    high = lax.ppermute(half[:RIM], "bfly", down)
    spread, low, high = lax.optimization_barrier((spread, low, high))

    crossed = pl.pallas_call(
        functools.partial(cross_kernel, levels),
        out_shape=jax.ShapeDtypeStruct((peers, depth, width), jnp.bfloat16),
        in_specs=[vmem(), vmem()],
        out_specs=vmem(),
        scratch_shapes=[pltpu.VMEM((peers, depth, 2 * width), jnp.bfloat16)],
        compiler_params=params(),
        cost_estimate=cost(levels * rows, 2 * width, width, 4 * rows * width),
        name="cross_levels",
    )(spread, stacked[LOCAL:])

    far = lax.all_to_all(crossed, "bfly", 0, 0, tiled=True).reshape(boxes, cols, width)


    near = pl.pallas_call(
        near_kernel,
        out_shape=jax.ShapeDtypeStruct((boxes, cols, width), jnp.float32),
        in_specs=[smem(), smem(), smem()] + [vmem()] * 5,
        out_specs=vmem(),
        scratch_shapes=[
            pltpu.VMEM((boxes + 2 * RIM, cols, width), jnp.bfloat16),
            pltpu.VMEM((boxes, cols, MAXB * width), jnp.bfloat16),
        ],
        compiler_params=params(),
        cost_estimate=cost(rows, MAXB * width, width, 8 * rows * width),
        name="near_field",
    )(
        (me * boxes)[None],
        near_cols,
        near_count,
        low,
        half,
        high,
        near_scale,
        table.reshape(8 * width, width),
    )

    mine = (far.astype(jnp.float32) + near).astype(jnp.bfloat16)
    other = lax.ppermute(mine, "sec", [(0, 1), (1, 0)])
    first = jnp.where(sec == 0, mine, other)
    second = jnp.where(sec == 0, other, mine)
    return jnp.concatenate([first, second], axis=1).astype(jnp.float32)


def solution(mesh):
    return jax.shard_map(
        shards,
        mesh=mesh,
        in_specs=(
            P("bfly", "probe", None),
            P(),
            P(None, "bfly", None),
            P(None, "bfly"),
            P("bfly"),
            P("bfly", None),
            P("bfly", None, None),
            P(None, "probe", None),
        ),
        out_specs=P("bfly", "probe", None),
        check_vma=False,
    )
```

```python
import functools

import jax
import jax.numpy as jnp
from jax import lax
from jax.experimental import pallas as pl
from jax.experimental.pallas import tpu as pltpu
from jax.sharding import PartitionSpec as P

LOCAL = 4
MAXB = 6
RIM = 8
VMEM_LIMIT = 40 * 1024 * 1024


def vmem():
    return pl.BlockSpec(memory_space=pltpu.VMEM)


def hbm():
    return pl.BlockSpec(memory_space=pltpu.HBM)


def smem():
    return pl.BlockSpec(memory_space=pltpu.SMEM)


def local_kernel(orders, which, probes, mixers, gains, out, half, weights, pairs, half_sem, sems):
    boxes, cols, width = out.shape
    columns = pl.ds(pl.multiple_of(which[0] * cols, cols), cols)
    fetch = pltpu.make_async_copy(probes.at[:, columns, :], half, half_sem)
    fetch.start()
    loads = [
        pltpu.make_async_copy(mixers.at[level], weights.at[level], sems.at[level])
        for level in range(LOCAL)
    ]
    for load in loads:
        load.start()
    fetch.wait()
    for level in range(LOCAL):
        source = half if level == 0 else out
        for box in range(boxes):
            block = source[orders[level, box]]
            pairs[box, :, :width] = block
            pairs[box ^ (1 << level), :, width:] = block
        loads[level].wait()
        mixed = jnp.dot(
            pairs[...].reshape(boxes * cols, 2 * width),
            weights[level],
            preferred_element_type=jnp.float32,
        ).reshape(boxes, cols, width)
        out[...] = (mixed * gains[level][:, None, :]).astype(out.dtype)


def cross_kernel(levels, rows, weights, out, pairs):
    count, depth, width = rows.shape
    for level in range(levels):
        source = rows if level == 0 else out
        for box in range(count):
            block = source[box]
            pairs[box, :, :width] = block
            pairs[box ^ (1 << level), :, width:] = block
        out[...] = (
            jnp.dot(
                pairs[...].reshape(count * depth, 2 * width),
                weights[level],
                preferred_element_type=jnp.float32,
            )
            .reshape(count, depth, width)
            .astype(out.dtype)
        )


def near_kernel(base, cols_ref, counts, low, own, high, scale, mine, other, out, extended, operand, table):
    boxes, cols, width = own.shape
    parts, slots, depth, _ = mine.shape
    for block, start in ((mine, base[1]), (other, base[2])):
        for part in range(parts):
            for slot in range(slots):
                at = pl.multiple_of(start + base[3 + part] + slot * width, depth)
                table[pl.ds(at, depth), :] = block[part, slot]
    extended[:RIM] = low[...]
    extended[RIM : RIM + boxes] = own[...]
    extended[RIM + boxes :] = high[...]
    first = base[0] - RIM
    for box in range(boxes):
        for slot in range(MAXB):
            block = extended[cols_ref[box, slot] - first].astype(jnp.float32)
            active = (slot < counts[box]).astype(jnp.float32)
            scaled = block * (scale[box, slot : slot + 1, :] * active)
            operand[box, :, slot * width : (slot + 1) * width] = scaled.astype(operand.dtype)
    out[...] = jnp.dot(
        operand[...].reshape(boxes * cols, MAXB * width),
        table[...],
        preferred_element_type=jnp.float32,
    ).reshape(boxes, cols, width)


def in_hbm(array):
    return pltpu.with_memory_space_constraint(array, pltpu.HBM)


def params():
    return pltpu.CompilerParams(vmem_limit_bytes=VMEM_LIMIT)


def cost(rows, depth, width, extra):
    return pl.CostEstimate(
        flops=2 * rows * depth * width, bytes_accessed=extra, transcendentals=0
    )


def shards(probes, mixers, box_gains, box_orders, near_count, near_cols, near_scale, near_table):
    boxes, columns, width = probes.shape
    peers = lax.axis_size("bfly")
    levels = mixers.shape[0] - LOCAL
    sec = lax.axis_index("sec")
    me = lax.axis_index("bfly")
    cols = columns // 2
    rows = boxes * cols
    depth = rows // peers
    stacked = mixers.reshape(mixers.shape[0], 2 * width, width)
    current = pl.pallas_call(
        local_kernel,
        out_shape=pltpu.HBM((boxes, cols, width), jnp.bfloat16),
        in_specs=[smem(), smem(), hbm(), hbm(), vmem()],
        out_specs=vmem(),
        scratch_shapes=[
            pltpu.VMEM((boxes, cols, width), jnp.bfloat16),
            pltpu.VMEM((LOCAL, 2 * width, width), jnp.bfloat16),
            pltpu.VMEM((boxes, cols, 2 * width), jnp.bfloat16),
            pltpu.SemaphoreType.DMA,
            pltpu.SemaphoreType.DMA((LOCAL,)),
        ],
        compiler_params=params(),
        cost_estimate=cost(LOCAL * rows, 2 * width, width, 4 * rows * width),
        name="local_levels",
    )(box_orders, sec[None], in_hbm(probes), in_hbm(stacked), box_gains)

    spread = lax.all_to_all(current.reshape(peers, depth, width), "bfly", 0, 0, tiled=True)

    half = lax.dynamic_slice_in_dim(probes, sec * cols, cols, axis=1)
    up = [(i, i + 1) for i in range(peers - 1)]
    down = [(i + 1, i) for i in range(peers - 1)]
    low = lax.ppermute(half[boxes - RIM :], "bfly", up)
    high = lax.ppermute(half[:RIM], "bfly", down)

    slots = MAXB // 2
    splits = lax.axis_size("probe")
    here = lax.axis_index("probe")
    table = lax.dynamic_slice_in_dim(near_table, sec * slots, slots, axis=0)[None]
    placed, step = [0], splits // 2
    while step:
        if step == 1:
            spread, low, high, table = lax.optimization_barrier((spread, low, high, table))
        got = lax.ppermute(table, "probe", [(i, i ^ step) for i in range(splits)])
        table = jnp.concatenate([table, got], axis=0)
        placed += [i ^ step for i in placed]
        step //= 2
    other_table = lax.ppermute(table, "sec", [(0, 1), (1, 0)])

    crossed = pl.pallas_call(
        functools.partial(cross_kernel, levels),
        out_shape=pltpu.HBM((peers, depth, width), jnp.bfloat16),
        in_specs=[vmem(), vmem()],
        out_specs=vmem(),
        scratch_shapes=[pltpu.VMEM((peers, depth, 2 * width), jnp.bfloat16)],
        compiler_params=params(),
        cost_estimate=cost(levels * rows, 2 * width, width, 4 * rows * width),
        name="cross_levels",
    )(spread, stacked[LOCAL:])

    far = lax.all_to_all(crossed, "bfly", 0, 0, tiled=True).reshape(boxes, cols, width)

    base = jnp.stack(
        [me * boxes, sec * (slots * width), (1 - sec) * (slots * width)]
        + [(here ^ i) * near_table.shape[1] for i in placed]
    )
    near = pl.pallas_call(
        near_kernel,
        out_shape=jax.ShapeDtypeStruct((boxes, cols, width), jnp.float32),
        in_specs=[smem(), smem(), smem()] + [vmem()] * 6,
        out_specs=vmem(),
        scratch_shapes=[
            pltpu.VMEM((boxes + 2 * RIM, cols, width), jnp.bfloat16),
            pltpu.VMEM((boxes, cols, MAXB * width), jnp.bfloat16),
            pltpu.VMEM((MAXB * width, width), jnp.bfloat16),
        ],
        compiler_params=params(),
        cost_estimate=cost(rows, MAXB * width, width, 8 * rows * width),
        name="near_field",
    )(base, near_cols, near_count, low, half, high, near_scale, table, other_table)

    mine = (far.astype(jnp.float32) + near).astype(jnp.bfloat16)
    other = lax.ppermute(mine, "sec", [(0, 1), (1, 0)])
    first = jnp.where(sec == 0, mine, other)
    second = jnp.where(sec == 0, other, mine)
    return jnp.concatenate([first, second], axis=1).astype(jnp.float32)


def solution(mesh):
    return jax.shard_map(
        shards,
        mesh=mesh,
        in_specs=(
            P("bfly", "probe", None),
            P(),
            P(None, "bfly", None),
            P(None, "bfly"),
            P("bfly"),
            P("bfly", None),
            P("bfly", None, None),
            P(None, "probe", None),
        ),
        out_specs=P("bfly", "probe", None),
        check_vma=False,
    )
```

```python
import functools

import jax
import jax.numpy as jnp
from jax import lax
from jax.experimental import pallas as pl
from jax.experimental.pallas import tpu as pltpu
from jax.sharding import PartitionSpec as P

LOCAL = 4
MAXB = 6
RIM = 8
VMEM_LIMIT = 40 * 1024 * 1024


def vmem():
    return pl.BlockSpec(memory_space=pltpu.VMEM)


def smem():
    return pl.BlockSpec(memory_space=pltpu.SMEM)


def hbm():
    return pl.BlockSpec(memory_space=pltpu.HBM)


def in_hbm(array):
    return pltpu.with_memory_space_constraint(array, pltpu.HBM)


def params():
    return pltpu.CompilerParams(vmem_limit_bytes=VMEM_LIMIT)


def cost(rows, depth, width, moved):
    return pl.CostEstimate(
        flops=2 * rows * depth * width, bytes_accessed=moved, transcendentals=0
    )


def local_kernel(
    orders_in, probes, mixers, gains_in, out, orders, gains, boxes_in, weights, pairs, sems, level_sems
):
    boxes, cols, width = out.shape
    fetches = [
        pltpu.make_async_copy(orders_in, orders, sems.at[0]),
        pltpu.make_async_copy(probes, boxes_in, sems.at[1]),
        pltpu.make_async_copy(gains_in, gains, sems.at[2]),
    ]
    loads = [
        pltpu.make_async_copy(mixers.at[level], weights.at[level], level_sems.at[level])
        for level in range(LOCAL)
    ]
    for copy in fetches + loads:
        copy.start()
    for copy in fetches:
        copy.wait()
    for level in range(LOCAL):
        source = boxes_in if level == 0 else out
        for box in range(boxes):
            block = source[orders[level, box]]
            pairs[box, :, :width] = block
            pairs[box ^ (1 << level), :, width:] = block
        loads[level].wait()
        mixed = jnp.dot(
            pairs[...].reshape(boxes * cols, 2 * width),
            weights[level],
            preferred_element_type=jnp.float32,
        ).reshape(boxes, cols, width)
        out[...] = (mixed * gains[level][:, None, :]).astype(out.dtype)


def cross_kernel(rows, mixers, out, weights, pairs, level_sems):
    count, depth, width = rows.shape
    levels = weights.shape[0]
    loads = [
        pltpu.make_async_copy(mixers.at[LOCAL + level], weights.at[level], level_sems.at[level])
        for level in range(levels)
    ]
    for copy in loads:
        copy.start()
    for level in range(levels):
        source = rows if level == 0 else out
        for box in range(count):
            block = source[box]
            pairs[box, :, :width] = block
            pairs[box ^ (1 << level), :, width:] = block
        loads[level].wait()
        mixed = jnp.dot(
            pairs[...].reshape(count * depth, 2 * width),
            weights[level],
            preferred_element_type=jnp.float32,
        )
        out[...] = mixed.reshape(count, depth, width).astype(out.dtype)


def near_kernel(base, cols_ref, counts, low, own, high, scale, table, out, extended, operand):
    boxes, cols, width = own.shape
    extended[:RIM] = low[...]
    extended[RIM : RIM + boxes] = own[...]
    extended[RIM + boxes :] = high[...]
    first = base[0] - RIM
    for box in range(boxes):
        for slot in range(MAXB):
            block = extended[cols_ref[box, slot] - first].astype(jnp.float32)
            active = (slot < counts[box]).astype(jnp.float32)
            scaled = block * (scale[box, slot : slot + 1, :] * active)
            operand[box, :, slot * width : (slot + 1) * width] = scaled.astype(operand.dtype)
    out[...] = (
        jnp.dot(
            operand[...].reshape(boxes * cols, MAXB * width),
            table[...],
            preferred_element_type=jnp.float32,
        )
        .reshape(boxes, cols, width)
        .astype(out.dtype)
    )


def shards(probes, mixers, box_gains, box_orders, near_count, near_cols, near_scale, near_table):
    boxes, cols, width = probes.shape
    peers = lax.axis_size("bfly")
    levels = mixers.shape[0] - LOCAL
    rows = boxes * cols
    depth = rows // peers
    is_far = lax.axis_index("sec") == 0
    stacked = mixers.reshape(mixers.shape[0], 2 * width, width)

    def far_term(probes):
        current = pl.pallas_call(
            local_kernel,
            out_shape=jax.ShapeDtypeStruct((boxes, cols, width), jnp.bfloat16),
            in_specs=[hbm(), hbm(), hbm(), hbm()],
            out_specs=vmem(),
            scratch_shapes=[
                pltpu.SMEM((LOCAL, boxes), jnp.int32),
                pltpu.VMEM((LOCAL, boxes, width), jnp.float32),
                pltpu.VMEM((boxes, cols, width), jnp.bfloat16),
                pltpu.VMEM((LOCAL, 2 * width, width), jnp.bfloat16),
                pltpu.VMEM((boxes, cols, 2 * width), jnp.bfloat16),
                pltpu.SemaphoreType.DMA((3,)),
                pltpu.SemaphoreType.DMA((LOCAL,)),
            ],
            compiler_params=params(),
            cost_estimate=cost(LOCAL * rows, 2 * width, width, 4 * rows * width),
            name="local_levels",
        )(in_hbm(box_orders), in_hbm(probes), in_hbm(stacked), in_hbm(box_gains))
        spread = lax.all_to_all(current.reshape(peers, depth, width), "bfly", 0, 0, tiled=True)
        crossed = pl.pallas_call(
            cross_kernel,
            out_shape=jax.ShapeDtypeStruct((peers, depth, width), jnp.bfloat16),
            in_specs=[vmem(), hbm()],
            out_specs=vmem(),
            scratch_shapes=[
                pltpu.VMEM((levels, 2 * width, width), jnp.bfloat16),
                pltpu.VMEM((peers, depth, 2 * width), jnp.bfloat16),
                pltpu.SemaphoreType.DMA((levels,)),
            ],
            compiler_params=params(),
            cost_estimate=cost(levels * rows, 2 * width, width, 4 * rows * width),
            name="cross_levels",
        )(spread, in_hbm(stacked))
        back = lax.all_to_all(crossed, "bfly", 0, 0, tiled=True)
        return back.reshape(boxes, cols, width)

    def near_term(probes):
        up = [(i, i + 1) for i in range(peers - 1)]
        down = [(i + 1, i) for i in range(peers - 1)]
        low = lax.ppermute(probes[boxes - RIM :], "bfly", up)
        high = lax.ppermute(probes[:RIM], "bfly", down)
        low, high, piece = lax.optimization_barrier((low, high, near_table))
        table = lax.all_gather(piece, "probe", axis=1, tiled=True)
        return pl.pallas_call(
            near_kernel,
            out_shape=jax.ShapeDtypeStruct((boxes, cols, width), jnp.bfloat16),
            in_specs=[smem(), smem(), smem()] + [vmem()] * 5,
            out_specs=vmem(),
            scratch_shapes=[
                pltpu.VMEM((boxes + 2 * RIM, cols, width), jnp.bfloat16),
                pltpu.VMEM((boxes, cols, MAXB * width), jnp.bfloat16),
            ],
            compiler_params=params(),
            cost_estimate=cost(rows, MAXB * width, width, 8 * rows * width),
            name="near_field",
        )(
            (lax.axis_index("bfly") * boxes)[None],
            near_cols,
            near_count,
            low,
            probes,
            high,
            near_scale,
            table.reshape(MAXB * width, width),
        )

    term = lax.cond(is_far, far_term, near_term, probes)
    other = lax.ppermute(term, "sec", [(0, 1), (1, 0)])
    return term.astype(jnp.float32) + other.astype(jnp.float32)


def solution(mesh):
    return jax.shard_map(
        shards,
        mesh=mesh,
        in_specs=(
            P("bfly", "probe", None),
            P(),
            P(None, "bfly", None),
            P(None, "bfly"),
            P("bfly"),
            P("bfly", None),
            P("bfly", None, None),
            P(None, "probe", None),
        ),
        out_specs=P("bfly", "probe", None),
        check_vma=False,
    )
```

```python
import functools

import jax
import jax.numpy as jnp
from jax import lax
from jax.experimental import pallas as pl
from jax.experimental.pallas import tpu as pltpu
from jax.sharding import PartitionSpec as P

LOCAL = 4
MAXB = 6
RIM = 8
LOCAL_TILE = 2
CROSS_TILE = 8
VMEM_LIMIT = 40 * 1024 * 1024


def vmem():
    return pl.BlockSpec(memory_space=pltpu.VMEM)


def smem():
    return pl.BlockSpec(memory_space=pltpu.SMEM)


def hbm():
    return pl.BlockSpec(memory_space=pltpu.HBM)


def in_hbm(array):
    return pltpu.with_memory_space_constraint(array, pltpu.HBM)


def params():
    return pltpu.CompilerParams(vmem_limit_bytes=VMEM_LIMIT)


def cost(rows, depth, width, moved):
    return pl.CostEstimate(
        flops=2 * rows * depth * width, bytes_accessed=moved, transcendentals=0
    )


def local_kernel(
    orders_in, probes, mixers, gains_in, out, orders, gains, boxes_in, weights, pairs, sems, level_sems
):
    boxes, cols, width = out.shape
    fetches = [
        pltpu.make_async_copy(orders_in, orders, sems.at[0]),
        pltpu.make_async_copy(probes, boxes_in, sems.at[1]),
        pltpu.make_async_copy(gains_in, gains, sems.at[2]),
    ]
    loads = [
        pltpu.make_async_copy(mixers.at[level], weights.at[level], level_sems.at[level])
        for level in range(LOCAL)
    ]
    for copy in fetches + loads:
        copy.start()
    for copy in fetches:
        copy.wait()
    for level in range(LOCAL):
        source = boxes_in if level == 0 else out
        for box in range(boxes):
            block = source[orders[level, box]]
            pairs[box, :, :width] = block
            pairs[box ^ (1 << level), :, width:] = block
        loads[level].wait()
        for start in range(0, boxes, LOCAL_TILE):
            tile = slice(start, start + LOCAL_TILE)
            mixed = jnp.dot(
                pairs[tile].reshape(LOCAL_TILE * cols, 2 * width),
                weights[level],
                preferred_element_type=jnp.float32,
            ).reshape(LOCAL_TILE, cols, width)
            out[tile] = (mixed * gains[level, tile][:, None, :]).astype(out.dtype)


def cross_kernel(rows, mixers, out, weights, pairs, level_sems):
    count, depth, width = rows.shape
    levels = weights.shape[0]
    loads = [
        pltpu.make_async_copy(mixers.at[LOCAL + level], weights.at[level], level_sems.at[level])
        for level in range(levels)
    ]
    for copy in loads:
        copy.start()
    for level in range(levels):
        source = rows if level == 0 else out
        for box in range(count):
            block = source[box]
            pairs[box, :, :width] = block
            pairs[box ^ (1 << level), :, width:] = block
        loads[level].wait()
        for start in range(0, count, CROSS_TILE):
            tile = slice(start, start + CROSS_TILE)
            mixed = jnp.dot(
                pairs[tile].reshape(CROSS_TILE * depth, 2 * width),
                weights[level],
                preferred_element_type=jnp.float32,
            )
            out[tile] = mixed.reshape(CROSS_TILE, depth, width).astype(out.dtype)


def near_kernel(base, cols_ref, counts, low, own, high, scale, table, out, extended, operand):
    boxes, cols, width = own.shape
    extended[:RIM] = low[...]
    extended[RIM : RIM + boxes] = own[...]
    extended[RIM + boxes :] = high[...]
    first = base[0] - RIM
    for box in range(boxes):
        for slot in range(MAXB):
            block = extended[cols_ref[box, slot] - first].astype(jnp.float32)
            active = (slot < counts[box]).astype(jnp.float32)
            scaled = block * (scale[box, slot : slot + 1, :] * active)
            operand[box, :, slot * width : (slot + 1) * width] = scaled.astype(operand.dtype)
    out[...] = (
        jnp.dot(
            operand[...].reshape(boxes * cols, MAXB * width),
            table[...],
            preferred_element_type=jnp.float32,
        )
        .reshape(boxes, cols, width)
        .astype(out.dtype)
    )


def shards(probes, mixers, box_gains, box_orders, near_count, near_cols, near_scale, near_table):
    boxes, cols, width = probes.shape
    peers = lax.axis_size("bfly")
    levels = mixers.shape[0] - LOCAL
    rows = boxes * cols
    depth = rows // peers
    is_far = lax.axis_index("sec") == 1
    stacked = mixers.reshape(mixers.shape[0], 2 * width, width)

    def far_term(probes):
        current = pl.pallas_call(
            local_kernel,
            out_shape=jax.ShapeDtypeStruct((boxes, cols, width), jnp.bfloat16),
            in_specs=[hbm(), hbm(), hbm(), hbm()],
            out_specs=vmem(),
            scratch_shapes=[
                pltpu.SMEM((LOCAL, boxes), jnp.int32),
                pltpu.VMEM((LOCAL, boxes, width), jnp.float32),
                pltpu.VMEM((boxes, cols, width), jnp.bfloat16),
                pltpu.VMEM((LOCAL, 2 * width, width), jnp.bfloat16),
                pltpu.VMEM((boxes, cols, 2 * width), jnp.bfloat16),
                pltpu.SemaphoreType.DMA((3,)),
                pltpu.SemaphoreType.DMA((LOCAL,)),
            ],
            compiler_params=params(),
            cost_estimate=cost(LOCAL * rows, 2 * width, width, 4 * rows * width),
            name="local_levels",
        )(in_hbm(box_orders), in_hbm(probes), in_hbm(stacked), in_hbm(box_gains))
        spread = lax.all_to_all(current.reshape(peers, depth, width), "bfly", 0, 0, tiled=True)
        crossed = pl.pallas_call(
            cross_kernel,
            out_shape=jax.ShapeDtypeStruct((peers, depth, width), jnp.bfloat16),
            in_specs=[vmem(), hbm()],
            out_specs=vmem(),
            scratch_shapes=[
                pltpu.VMEM((levels, 2 * width, width), jnp.bfloat16),
                pltpu.VMEM((peers, depth, 2 * width), jnp.bfloat16),
                pltpu.SemaphoreType.DMA((levels,)),
            ],
            compiler_params=params(),
            cost_estimate=cost(levels * rows, 2 * width, width, 4 * rows * width),
            name="cross_levels",
        )(spread, in_hbm(stacked))
        back = lax.all_to_all(crossed, "bfly", 0, 0, tiled=True)
        return back.reshape(boxes, cols, width)

    def near_term(probes):
        up = [(i, i + 1) for i in range(peers - 1)]
        down = [(i + 1, i) for i in range(peers - 1)]
        low = lax.ppermute(probes[boxes - RIM :], "bfly", up)
        high = lax.ppermute(probes[:RIM], "bfly", down)
        low, high, piece = lax.optimization_barrier((low, high, near_table))
        table = lax.all_gather(piece, "probe", axis=1, tiled=True)
        return pl.pallas_call(
            near_kernel,
            out_shape=jax.ShapeDtypeStruct((boxes, cols, width), jnp.bfloat16),
            in_specs=[smem(), smem(), smem()] + [vmem()] * 5,
            out_specs=vmem(),
            scratch_shapes=[
                pltpu.VMEM((boxes + 2 * RIM, cols, width), jnp.bfloat16),
                pltpu.VMEM((boxes, cols, MAXB * width), jnp.bfloat16),
            ],
            compiler_params=params(),
            cost_estimate=cost(rows, MAXB * width, width, 8 * rows * width),
            name="near_field",
        )(
            (lax.axis_index("bfly") * boxes)[None],
            near_cols,
            near_count,
            low,
            probes,
            high,
            near_scale,
            table.reshape(MAXB * width, width),
        )

    term = lax.cond(is_far, far_term, near_term, probes)
    other = lax.ppermute(term, "sec", [(0, 1), (1, 0)])
    term = lax.optimization_barrier(term)
    return term.astype(jnp.float32) + other.astype(jnp.float32)


def solution(mesh):
    return jax.shard_map(
        shards,
        mesh=mesh,
        in_specs=(
            P("bfly", "probe", None),
            P(),
            P(None, "bfly", None),
            P(None, "bfly"),
            P("bfly"),
            P("bfly", None),
            P("bfly", None, None),
            P(None, "probe", None),
        ),
        out_specs=P("bfly", "probe", None),
        check_vma=False,
    )
```

```python
import functools

import jax
import jax.numpy as jnp
from jax import lax
from jax.experimental import pallas as pl
from jax.experimental.pallas import tpu as pltpu
from jax.sharding import PartitionSpec as P

LOCAL = 4
MAXB = 6
RIM = 8
LOCAL_TILE = 2
CROSS_TILE = 8
VMEM_LIMIT = 40 * 1024 * 1024


def vmem():
    return pl.BlockSpec(memory_space=pltpu.VMEM)


def smem():
    return pl.BlockSpec(memory_space=pltpu.SMEM)


def hbm():
    return pl.BlockSpec(memory_space=pltpu.HBM)


def in_hbm(array):
    return pltpu.with_memory_space_constraint(array, pltpu.HBM)


def params():
    return pltpu.CompilerParams(vmem_limit_bytes=VMEM_LIMIT)


def cost(rows, depth, width, moved):
    return pl.CostEstimate(
        flops=2 * rows * depth * width, bytes_accessed=moved, transcendentals=0
    )


def local_kernel(
    orders_in, probes, mixers, gains_in, out, orders, gains, boxes_in, weights, pairs, sems, level_sems
):
    boxes, cols, width = out.shape
    fetches = [
        pltpu.make_async_copy(orders_in, orders, sems.at[0]),
        pltpu.make_async_copy(probes, boxes_in, sems.at[1]),
        pltpu.make_async_copy(gains_in, gains, sems.at[2]),
    ]
    loads = [
        pltpu.make_async_copy(mixers.at[level], weights.at[level], level_sems.at[level])
        for level in range(LOCAL)
    ]
    for copy in fetches + loads:
        copy.start()
    for copy in fetches:
        copy.wait()
    for level in range(LOCAL):
        source = boxes_in if level == 0 else out
        for box in range(boxes):
            block = source[orders[level, box]]
            pairs[box, :, :width] = block
            pairs[box ^ (1 << level), :, width:] = block
        loads[level].wait()
        for start in range(0, boxes, LOCAL_TILE):
            tile = slice(start, start + LOCAL_TILE)
            mixed = jnp.dot(
                pairs[tile].reshape(LOCAL_TILE * cols, 2 * width),
                weights[level],
                preferred_element_type=jnp.float32,
            ).reshape(LOCAL_TILE, cols, width)
            out[tile] = (mixed * gains[level, tile][:, None, :]).astype(out.dtype)


def cross_kernel(rows, mixers, out, pairs):
    count, depth, width = rows.shape
    levels = mixers.shape[0] - LOCAL
    for level in range(levels):
        source = rows if level == 0 else out
        for box in range(count):
            block = source[box]
            pairs[box, :, :width] = block
            pairs[box ^ (1 << level), :, width:] = block
        for start in range(0, count, CROSS_TILE):
            tile = slice(start, start + CROSS_TILE)
            mixed = jnp.dot(
                pairs[tile].reshape(CROSS_TILE * depth, 2 * width),
                mixers[LOCAL + level],
                preferred_element_type=jnp.float32,
            )
            out[tile] = mixed.reshape(CROSS_TILE, depth, width).astype(out.dtype)


def near_kernel(base, cols_ref, counts, low, own, high, scale, table, out, extended, operand):
    boxes, cols, width = own.shape
    extended[:RIM] = low[...]
    extended[RIM : RIM + boxes] = own[...]
    extended[RIM + boxes :] = high[...]
    first = base[0] - RIM
    for box in range(boxes):
        for slot in range(MAXB):
            block = extended[cols_ref[box, slot] - first].astype(jnp.float32)
            active = (slot < counts[box]).astype(jnp.float32)
            scaled = block * (scale[box, slot : slot + 1, :] * active)
            operand[box, :, slot * width : (slot + 1) * width] = scaled.astype(operand.dtype)
    out[...] = (
        jnp.dot(
            operand[...].reshape(boxes * cols, MAXB * width),
            table[...],
            preferred_element_type=jnp.float32,
        )
        .reshape(boxes, cols, width)
        .astype(out.dtype)
    )


def shards(probes, mixers, box_gains, box_orders, near_count, near_cols, near_scale, near_table):
    boxes, cols, width = probes.shape
    peers = lax.axis_size("bfly")
    levels = mixers.shape[0] - LOCAL
    rows = boxes * cols
    depth = rows // peers
    is_far = lax.axis_index("sec") == 1
    stacked = mixers.reshape(mixers.shape[0], 2 * width, width)

    def far_term(probes):
        current = pl.pallas_call(
            local_kernel,
            out_shape=jax.ShapeDtypeStruct((boxes, cols, width), jnp.bfloat16),
            in_specs=[hbm(), hbm(), hbm(), hbm()],
            out_specs=vmem(),
            scratch_shapes=[
                pltpu.SMEM((LOCAL, boxes), jnp.int32),
                pltpu.VMEM((LOCAL, boxes, width), jnp.float32),
                pltpu.VMEM((boxes, cols, width), jnp.bfloat16),
                pltpu.VMEM((LOCAL, 2 * width, width), jnp.bfloat16),
                pltpu.VMEM((boxes, cols, 2 * width), jnp.bfloat16),
                pltpu.SemaphoreType.DMA((3,)),
                pltpu.SemaphoreType.DMA((LOCAL,)),
            ],
            compiler_params=params(),
            cost_estimate=cost(LOCAL * rows, 2 * width, width, 4 * rows * width),
            name="local_levels",
        )(in_hbm(box_orders), in_hbm(probes), in_hbm(stacked), in_hbm(box_gains))
        spread = lax.all_to_all(current.reshape(peers, depth, width), "bfly", 0, 0, tiled=True)
        crossed = pl.pallas_call(
            cross_kernel,
            out_shape=jax.ShapeDtypeStruct((peers, depth, width), jnp.bfloat16),
            in_specs=[vmem(), vmem()],
            out_specs=vmem(),
            scratch_shapes=[pltpu.VMEM((peers, depth, 2 * width), jnp.bfloat16)],
            compiler_params=params(),
            cost_estimate=cost(levels * rows, 2 * width, width, 4 * rows * width),
            name="cross_levels",
        )(spread, stacked)
        back = lax.all_to_all(crossed, "bfly", 0, 0, tiled=True)
        return back.reshape(boxes, cols, width)

    def near_term(probes):
        up = [(i, i + 1) for i in range(peers - 1)]
        down = [(i + 1, i) for i in range(peers - 1)]
        table = lax.all_gather(near_table, "probe", axis=1, tiled=True)
        table, lower, upper = lax.optimization_barrier((table, probes[boxes - RIM :], probes[:RIM]))
        low = lax.ppermute(lower, "bfly", up)
        high = lax.ppermute(upper, "bfly", down)
        return pl.pallas_call(
            near_kernel,
            out_shape=pltpu.VMEM((boxes, cols, width), jnp.bfloat16),
            in_specs=[smem(), smem(), smem()] + [vmem()] * 5,
            out_specs=vmem(),
            scratch_shapes=[
                pltpu.VMEM((boxes + 2 * RIM, cols, width), jnp.bfloat16),
                pltpu.VMEM((boxes, cols, MAXB * width), jnp.bfloat16),
            ],
            compiler_params=params(),
            cost_estimate=cost(rows, MAXB * width, width, 8 * rows * width),
            name="near_field",
        )(
            (lax.axis_index("bfly") * boxes)[None],
            near_cols,
            near_count,
            low,
            probes,
            high,
            near_scale,
            table.reshape(MAXB * width, width),
        )

    term = lax.cond(is_far, far_term, near_term, probes)
    other = lax.ppermute(term, "sec", [(0, 1), (1, 0)])
    term = lax.optimization_barrier(term)
    return term.astype(jnp.float32) + other.astype(jnp.float32)


def solution(mesh):
    return jax.shard_map(
        shards,
        mesh=mesh,
        in_specs=(
            P("bfly", "probe", None),
            P(),
            P(None, "bfly", None),
            P(None, "bfly"),
            P("bfly"),
            P("bfly", None),
            P("bfly", None, None),
            P(None, "probe", None),
        ),
        out_specs=P("bfly", "probe", None),
        check_vma=False,
    )
```

```python
import functools

import jax
import jax.numpy as jnp
from jax import lax
from jax.experimental import pallas as pl
from jax.experimental.pallas import tpu as pltpu
from jax.sharding import PartitionSpec as P

LOCAL = 4
MAXB = 6
RIM = 8
LOCAL_TILE = 2
CROSS_TILE = 8
VMEM_LIMIT = 40 * 1024 * 1024


def vmem():
    return pl.BlockSpec(memory_space=pltpu.VMEM)


def smem():
    return pl.BlockSpec(memory_space=pltpu.SMEM)


def hbm():
    return pl.BlockSpec(memory_space=pltpu.HBM)


def in_hbm(array):
    return pltpu.with_memory_space_constraint(array, pltpu.HBM)


def params():
    return pltpu.CompilerParams(vmem_limit_bytes=VMEM_LIMIT)


def cost(rows, depth, width, moved):
    return pl.CostEstimate(
        flops=2 * rows * depth * width, bytes_accessed=moved, transcendentals=0
    )


def local_kernel(
    orders_in, probes, mixers, gains_in, out, orders, gains, boxes_in, weights, pairs, sems, level_sems
):
    boxes, cols, width = out.shape
    fetches = [
        pltpu.make_async_copy(orders_in, orders, sems.at[0]),
        pltpu.make_async_copy(probes, boxes_in, sems.at[1]),
        pltpu.make_async_copy(gains_in, gains, sems.at[2]),
    ]
    loads = [
        pltpu.make_async_copy(mixers.at[level], weights.at[level], level_sems.at[level])
        for level in range(LOCAL)
    ]
    for copy in fetches + loads:
        copy.start()
    for copy in fetches:
        copy.wait()
    for level in range(LOCAL):
        source = boxes_in if level == 0 else out
        for box in range(boxes):
            block = source[orders[level, box]]
            pairs[box, :, :width] = block
            pairs[box ^ (1 << level), :, width:] = block
        loads[level].wait()
        for start in range(0, boxes, LOCAL_TILE):
            tile = slice(start, start + LOCAL_TILE)
            mixed = jnp.dot(
                pairs[tile].reshape(LOCAL_TILE * cols, 2 * width),
                weights[level],
                preferred_element_type=jnp.float32,
            ).reshape(LOCAL_TILE, cols, width)
            out[tile] = (mixed * gains[level, tile][:, None, :]).astype(out.dtype)


def cross_kernel(rows, mixers, out, pairs):
    count, depth, width = rows.shape
    levels = mixers.shape[0] - LOCAL
    for level in range(levels):
        source = rows if level == 0 else out
        for box in range(count):
            block = source[box]
            pairs[box, :, :width] = block
            pairs[box ^ (1 << level), :, width:] = block
        for start in range(0, count, CROSS_TILE):
            tile = slice(start, start + CROSS_TILE)
            mixed = jnp.dot(
                pairs[tile].reshape(CROSS_TILE * depth, 2 * width),
                mixers[LOCAL + level],
                preferred_element_type=jnp.float32,
            )
            out[tile] = mixed.reshape(CROSS_TILE, depth, width).astype(out.dtype)


def near_kernel(base, cols_ref, counts, low, own, high, scale, parts, out, extended, operand, table):
    boxes, cols, width = own.shape
    splits, slots, depth, _ = parts.shape
    for split in range(splits):
        for slot in range(slots):
            start = slot * width + split * depth
            table[start : start + depth] = parts[split, slot]
    extended[:RIM] = low[...]
    extended[RIM : RIM + boxes] = own[...]
    extended[RIM + boxes :] = high[...]
    first = base[0] - RIM
    for box in range(boxes):
        for slot in range(MAXB):
            block = extended[cols_ref[box, slot] - first].astype(jnp.float32)
            active = (slot < counts[box]).astype(jnp.float32)
            scaled = block * (scale[box, slot : slot + 1, :] * active)
            operand[box, :, slot * width : (slot + 1) * width] = scaled.astype(operand.dtype)
    out[...] = (
        jnp.dot(
            operand[...].reshape(boxes * cols, MAXB * width),
            table[...],
            preferred_element_type=jnp.float32,
        )
        .reshape(boxes, cols, width)
        .astype(out.dtype)
    )


def shards(probes, mixers, box_gains, box_orders, near_count, near_cols, near_scale, near_table):
    boxes, cols, width = probes.shape
    peers = lax.axis_size("bfly")
    levels = mixers.shape[0] - LOCAL
    rows = boxes * cols
    depth = rows // peers
    is_far = lax.axis_index("sec") == 1
    stacked = mixers.reshape(mixers.shape[0], 2 * width, width)

    def far_term(probes):
        current = pl.pallas_call(
            local_kernel,
            out_shape=jax.ShapeDtypeStruct((boxes, cols, width), jnp.bfloat16),
            in_specs=[hbm(), hbm(), hbm(), hbm()],
            out_specs=vmem(),
            scratch_shapes=[
                pltpu.SMEM((LOCAL, boxes), jnp.int32),
                pltpu.VMEM((LOCAL, boxes, width), jnp.float32),
                pltpu.VMEM((boxes, cols, width), jnp.bfloat16),
                pltpu.VMEM((LOCAL, 2 * width, width), jnp.bfloat16),
                pltpu.VMEM((boxes, cols, 2 * width), jnp.bfloat16),
                pltpu.SemaphoreType.DMA((3,)),
                pltpu.SemaphoreType.DMA((LOCAL,)),
            ],
            compiler_params=params(),
            cost_estimate=cost(LOCAL * rows, 2 * width, width, 4 * rows * width),
            name="local_levels",
        )(in_hbm(box_orders), in_hbm(probes), in_hbm(stacked), in_hbm(box_gains))
        current, later = lax.optimization_barrier((current, stacked))
        spread = lax.all_to_all(current.reshape(peers, depth, width), "bfly", 0, 0, tiled=True)
        crossed = pl.pallas_call(
            cross_kernel,
            out_shape=jax.ShapeDtypeStruct((peers, depth, width), jnp.bfloat16),
            in_specs=[vmem(), vmem()],
            out_specs=vmem(),
            scratch_shapes=[pltpu.VMEM((peers, depth, 2 * width), jnp.bfloat16)],
            compiler_params=params(),
            cost_estimate=cost(levels * rows, 2 * width, width, 4 * rows * width),
            name="cross_levels",
        )(spread, later)
        back = lax.all_to_all(crossed, "bfly", 0, 0, tiled=True)
        return back.reshape(boxes, cols, width)

    def near_term(probes):
        up = [(i, i + 1) for i in range(peers - 1)]
        down = [(i + 1, i) for i in range(peers - 1)]
        low = lax.ppermute(probes[boxes - RIM :], "bfly", up)
        high = lax.ppermute(probes[:RIM], "bfly", down)
        low, high, piece = lax.optimization_barrier((low, high, near_table))
        copies = jnp.broadcast_to(piece, (lax.axis_size("probe"), *piece.shape))
        parts = lax.all_to_all(copies, "probe", 0, 0, tiled=True)
        return pl.pallas_call(
            near_kernel,
            out_shape=pltpu.VMEM((boxes, cols, width), jnp.bfloat16),
            in_specs=[smem(), smem(), smem()] + [vmem()] * 5,
            out_specs=vmem(),
            scratch_shapes=[
                pltpu.VMEM((boxes + 2 * RIM, cols, width), jnp.bfloat16),
                pltpu.VMEM((boxes, cols, MAXB * width), jnp.bfloat16),
                pltpu.VMEM((MAXB * width, width), jnp.bfloat16),
            ],
            compiler_params=params(),
            cost_estimate=cost(rows, MAXB * width, width, 8 * rows * width),
            name="near_field",
        )(
            (lax.axis_index("bfly") * boxes)[None],
            near_cols,
            near_count,
            low,
            probes,
            high,
            near_scale,
            parts,
        )

    term = lax.cond(is_far, far_term, near_term, probes)
    other = lax.ppermute(term, "sec", [(0, 1), (1, 0)])
    term = lax.optimization_barrier(term)
    return term.astype(jnp.float32) + other.astype(jnp.float32)


def solution(mesh):
    return jax.shard_map(
        shards,
        mesh=mesh,
        in_specs=(
            P("bfly", "probe", None),
            P(),
            P(None, "bfly", None),
            P(None, "bfly"),
            P("bfly"),
            P("bfly", None),
            P("bfly", None, None),
            P(None, "probe", None),
        ),
        out_specs=P("bfly", "probe", None),
        check_vma=False,
    )
```

```python
import functools

import jax
import jax.numpy as jnp
from jax import lax
from jax.experimental import pallas as pl
from jax.experimental.pallas import tpu as pltpu
from jax.sharding import PartitionSpec as P

LOCAL = 4
MAXB = 6
RIM = 8
LOCAL_TILE = 2
CROSS_TILE = 8
VMEM_LIMIT = 40 * 1024 * 1024


def vmem():
    return pl.BlockSpec(memory_space=pltpu.VMEM)


def smem():
    return pl.BlockSpec(memory_space=pltpu.SMEM)


def hbm():
    return pl.BlockSpec(memory_space=pltpu.HBM)


def in_hbm(array):
    return pltpu.with_memory_space_constraint(array, pltpu.HBM)


def params():
    return pltpu.CompilerParams(vmem_limit_bytes=VMEM_LIMIT)


def cost(rows, depth, width, moved):
    return pl.CostEstimate(
        flops=2 * rows * depth * width, bytes_accessed=moved, transcendentals=0
    )


def local_kernel(
    orders_in, probes, mixers, gains_in, out, orders, gains, boxes_in, weights, pairs, sems, level_sems
):
    boxes, cols, width = out.shape
    fetches = [
        pltpu.make_async_copy(orders_in, orders, sems.at[0]),
        pltpu.make_async_copy(probes, boxes_in, sems.at[1]),
        pltpu.make_async_copy(gains_in, gains, sems.at[2]),
    ]
    loads = [
        pltpu.make_async_copy(mixers.at[level], weights.at[level], level_sems.at[level])
        for level in range(LOCAL)
    ]
    for copy in fetches + loads:
        copy.start()
    for copy in fetches:
        copy.wait()
    for level in range(LOCAL):
        source = boxes_in if level == 0 else out
        for box in range(boxes):
            block = source[orders[level, box]]
            pairs[box, :, :width] = block
            pairs[box ^ (1 << level), :, width:] = block
        loads[level].wait()
        for start in range(0, boxes, LOCAL_TILE):
            tile = slice(start, start + LOCAL_TILE)
            mixed = jnp.dot(
                pairs[tile].reshape(LOCAL_TILE * cols, 2 * width),
                weights[level],
                preferred_element_type=jnp.float32,
            ).reshape(LOCAL_TILE, cols, width)
            out[tile] = (mixed * gains[level, tile][:, None, :]).astype(out.dtype)


def cross_kernel(rows, mixers, out, pairs):
    count, depth, width = rows.shape
    levels = mixers.shape[0] - LOCAL
    for level in range(levels):
        source = rows if level == 0 else out
        for box in range(count):
            block = source[box]
            pairs[box, :, :width] = block
            pairs[box ^ (1 << level), :, width:] = block
        for start in range(0, count, CROSS_TILE):
            tile = slice(start, start + CROSS_TILE)
            mixed = jnp.dot(
                pairs[tile].reshape(CROSS_TILE * depth, 2 * width),
                mixers[LOCAL + level],
                preferred_element_type=jnp.float32,
            )
            out[tile] = mixed.reshape(CROSS_TILE, depth, width).astype(out.dtype)


def near_kernel(base, cols_ref, counts, low, own, high, scale, parts, out, extended, operand, table):
    boxes, cols, width = own.shape
    splits, slots, depth, _ = parts.shape
    for split in range(splits):
        for slot in range(slots):
            start = slot * width + split * depth
            table[start : start + depth] = parts[split, slot]
    extended[:RIM] = low[...]
    extended[RIM : RIM + boxes] = own[...]
    extended[RIM + boxes :] = high[...]
    first = base[0] - RIM
    for box in range(boxes):
        for slot in range(MAXB):
            block = extended[cols_ref[box, slot] - first].astype(jnp.float32)
            active = (slot < counts[box]).astype(jnp.float32)
            scaled = block * (scale[box, slot : slot + 1, :] * active)
            operand[box, :, slot * width : (slot + 1) * width] = scaled.astype(operand.dtype)
    out[...] = (
        jnp.dot(
            operand[...].reshape(boxes * cols, MAXB * width),
            table[...],
            preferred_element_type=jnp.float32,
        )
        .reshape(boxes, cols, width)
        .astype(out.dtype)
    )


def shards(probes, mixers, box_gains, box_orders, near_count, near_cols, near_scale, near_table):
    boxes, cols, width = probes.shape
    peers = lax.axis_size("bfly")
    levels = mixers.shape[0] - LOCAL
    rows = boxes * cols
    depth = rows // peers
    is_far = lax.axis_index("sec") == 1
    stacked = mixers.reshape(mixers.shape[0], 2 * width, width)

    def far_term(probes):
        current = pl.pallas_call(
            local_kernel,
            out_shape=jax.ShapeDtypeStruct((boxes, cols, width), jnp.bfloat16),
            in_specs=[hbm(), hbm(), hbm(), hbm()],
            out_specs=vmem(),
            scratch_shapes=[
                pltpu.SMEM((LOCAL, boxes), jnp.int32),
                pltpu.VMEM((LOCAL, boxes, width), jnp.float32),
                pltpu.VMEM((boxes, cols, width), jnp.bfloat16),
                pltpu.VMEM((LOCAL, 2 * width, width), jnp.bfloat16),
                pltpu.VMEM((boxes, cols, 2 * width), jnp.bfloat16),
                pltpu.SemaphoreType.DMA((3,)),
                pltpu.SemaphoreType.DMA((LOCAL,)),
            ],
            compiler_params=params(),
            cost_estimate=cost(LOCAL * rows, 2 * width, width, 4 * rows * width),
            name="local_levels",
        )(in_hbm(box_orders), in_hbm(probes), in_hbm(stacked), in_hbm(box_gains))
        current, later = lax.optimization_barrier((current, stacked))
        spread = lax.all_to_all(current.reshape(peers, depth, width), "bfly", 0, 0, tiled=True)
        crossed = pl.pallas_call(
            cross_kernel,
            out_shape=jax.ShapeDtypeStruct((peers, depth, width), jnp.bfloat16),
            in_specs=[vmem(), vmem()],
            out_specs=vmem(),
            scratch_shapes=[pltpu.VMEM((peers, depth, 2 * width), jnp.bfloat16)],
            compiler_params=params(),
            cost_estimate=cost(levels * rows, 2 * width, width, 4 * rows * width),
            name="cross_levels",
        )(spread, later)
        back = lax.all_to_all(crossed, "bfly", 0, 0, tiled=True)
        return back.reshape(boxes, cols, width)

    def near_term(probes):
        up = [(i, i + 1) for i in range(peers - 1)]
        down = [(i + 1, i) for i in range(peers - 1)]
        low = lax.ppermute(probes[boxes - RIM :], "bfly", up)
        high = lax.ppermute(probes[:RIM], "bfly", down)
        copies = jnp.broadcast_to(near_table, (lax.axis_size("probe"), *near_table.shape))
        parts = lax.all_to_all(copies, "probe", 0, 0, tiled=True)
        return pl.pallas_call(
            near_kernel,
            out_shape=pltpu.VMEM((boxes, cols, width), jnp.bfloat16),
            in_specs=[smem(), smem(), smem()] + [vmem()] * 5,
            out_specs=vmem(),
            scratch_shapes=[
                pltpu.VMEM((boxes + 2 * RIM, cols, width), jnp.bfloat16),
                pltpu.VMEM((boxes, cols, MAXB * width), jnp.bfloat16),
                pltpu.VMEM((MAXB * width, width), jnp.bfloat16),
            ],
            compiler_params=params(),
            cost_estimate=cost(rows, MAXB * width, width, 8 * rows * width),
            name="near_field",
        )(
            (lax.axis_index("bfly") * boxes)[None],
            near_cols,
            near_count,
            low,
            probes,
            high,
            near_scale,
            parts,
        )

    term = lax.cond(is_far, far_term, near_term, probes)
    other = lax.ppermute(term, "sec", [(0, 1), (1, 0)])
    term = lax.optimization_barrier(term)
    return term.astype(jnp.float32) + other.astype(jnp.float32)


def solution(mesh):
    return jax.shard_map(
        shards,
        mesh=mesh,
        in_specs=(
            P("bfly", "probe", None),
            P(),
            P(None, "bfly", None),
            P(None, "bfly"),
            P("bfly"),
            P("bfly", None),
            P("bfly", None, None),
            P(None, "probe", None),
        ),
        out_specs=P("bfly", "probe", None),
        check_vma=False,
    )
```

```python
import functools

import jax
import jax.numpy as jnp
from jax import lax
from jax.experimental import pallas as pl
from jax.experimental.pallas import tpu as pltpu
from jax.sharding import PartitionSpec as P

LOCAL = 4
MAXB = 6
RIM = 8
LOCAL_TILE = 2
CROSS_TILE = 8
VMEM_LIMIT = 40 * 1024 * 1024


def vmem():
    return pl.BlockSpec(memory_space=pltpu.VMEM)


def smem():
    return pl.BlockSpec(memory_space=pltpu.SMEM)


def hbm():
    return pl.BlockSpec(memory_space=pltpu.HBM)


def in_hbm(array):
    return pltpu.with_memory_space_constraint(array, pltpu.HBM)


def params():
    return pltpu.CompilerParams(vmem_limit_bytes=VMEM_LIMIT)


def cost(rows, depth, width, moved):
    return pl.CostEstimate(
        flops=2 * rows * depth * width, bytes_accessed=moved, transcendentals=0
    )


def local_kernel(
    orders_in, probes, mixers, gains_in, out, orders, gains, boxes_in, weights, pairs, sems, level_sems
):
    boxes, cols, width = out.shape
    fetches = [
        pltpu.make_async_copy(orders_in, orders, sems.at[0]),
        pltpu.make_async_copy(probes, boxes_in, sems.at[1]),
        pltpu.make_async_copy(gains_in, gains, sems.at[2]),
    ]
    loads = [
        pltpu.make_async_copy(mixers.at[level], weights.at[level], level_sems.at[level])
        for level in range(LOCAL)
    ]
    for copy in fetches + loads:
        copy.start()
    for copy in fetches:
        copy.wait()
    for level in range(LOCAL):
        source = boxes_in if level == 0 else out
        for box in range(boxes):
            block = source[orders[level, box]]
            pairs[box, :, :width] = block
            pairs[box ^ (1 << level), :, width:] = block
        loads[level].wait()
        for start in range(0, boxes, LOCAL_TILE):
            tile = slice(start, start + LOCAL_TILE)
            mixed = jnp.dot(
                pairs[tile].reshape(LOCAL_TILE * cols, 2 * width),
                weights[level],
                preferred_element_type=jnp.float32,
            ).reshape(LOCAL_TILE, cols, width)
            out[tile] = (mixed * gains[level, tile][:, None, :]).astype(out.dtype)


def cross_kernel(rows, mixers, out, pairs):
    count, depth, width = rows.shape
    levels = mixers.shape[0] - LOCAL
    for level in range(levels):
        source = rows if level == 0 else out
        for box in range(count):
            block = source[box]
            pairs[box, :, :width] = block
            pairs[box ^ (1 << level), :, width:] = block
        for start in range(0, count, CROSS_TILE):
            tile = slice(start, start + CROSS_TILE)
            mixed = jnp.dot(
                pairs[tile].reshape(CROSS_TILE * depth, 2 * width),
                mixers[LOCAL + level],
                preferred_element_type=jnp.float32,
            )
            out[tile] = mixed.reshape(CROSS_TILE, depth, width).astype(out.dtype)


def near_kernel(base, cols_ref, counts, low, own, high, scale, parts, out, extended, operand, table):
    boxes, cols, width = own.shape
    splits, slots, depth, _ = parts.shape
    for split in range(splits):
        for slot in range(slots):
            start = slot * width + split * depth
            table[start : start + depth] = parts[split, slot]
    extended[:RIM] = low[...]
    extended[RIM : RIM + boxes] = own[...]
    extended[RIM + boxes :] = high[...]
    first = base[0] - RIM
    for box in range(boxes):
        for slot in range(MAXB):
            block = extended[cols_ref[box, slot] - first].astype(jnp.float32)
            active = (slot < counts[box]).astype(jnp.float32)
            scaled = block * (scale[box, slot : slot + 1, :] * active)
            operand[box, :, slot * width : (slot + 1) * width] = scaled.astype(operand.dtype)
    out[...] = (
        jnp.dot(
            operand[...].reshape(boxes * cols, MAXB * width),
            table[...],
            preferred_element_type=jnp.float32,
        )
        .reshape(boxes, cols, width)
        .astype(out.dtype)
    )


def shards(probes, mixers, box_gains, box_orders, near_count, near_cols, near_scale, near_table):
    boxes, cols, width = probes.shape
    peers = lax.axis_size("bfly")
    levels = mixers.shape[0] - LOCAL
    rows = boxes * cols
    depth = rows // peers
    is_far = lax.axis_index("sec") == 1
    stacked = mixers.reshape(mixers.shape[0], 2 * width, width)

    def far_term(probes):
        current = pl.pallas_call(
            local_kernel,
            out_shape=jax.ShapeDtypeStruct((boxes, cols, width), jnp.bfloat16),
            in_specs=[hbm(), hbm(), hbm(), hbm()],
            out_specs=vmem(),
            scratch_shapes=[
                pltpu.SMEM((LOCAL, boxes), jnp.int32),
                pltpu.VMEM((LOCAL, boxes, width), jnp.float32),
                pltpu.VMEM((boxes, cols, width), jnp.bfloat16),
                pltpu.VMEM((LOCAL, 2 * width, width), jnp.bfloat16),
                pltpu.VMEM((boxes, cols, 2 * width), jnp.bfloat16),
                pltpu.SemaphoreType.DMA((3,)),
                pltpu.SemaphoreType.DMA((LOCAL,)),
            ],
            compiler_params=params(),
            cost_estimate=cost(LOCAL * rows, 2 * width, width, 4 * rows * width),
            name="local_levels",
        )(in_hbm(box_orders), in_hbm(probes), in_hbm(stacked), in_hbm(box_gains))
        current, later = lax.optimization_barrier((current, stacked))
        spread = lax.all_to_all(current.reshape(peers, depth, width), "bfly", 0, 0, tiled=True)
        crossed = pl.pallas_call(
            cross_kernel,
            out_shape=jax.ShapeDtypeStruct((peers, depth, width), jnp.bfloat16),
            in_specs=[vmem(), vmem()],
            out_specs=vmem(),
            scratch_shapes=[pltpu.VMEM((peers, depth, 2 * width), jnp.bfloat16)],
            compiler_params=params(),
            cost_estimate=cost(levels * rows, 2 * width, width, 4 * rows * width),
            name="cross_levels",
        )(spread, later)
        back = lax.all_to_all(crossed, "bfly", 0, 0, tiled=True)
        return back.reshape(boxes, cols, width)

    def near_term(probes):
        up = [(i, i + 1) for i in range(peers - 1)]
        down = [(i + 1, i) for i in range(peers - 1)]
        copies = jnp.broadcast_to(near_table, (lax.axis_size("probe"), *near_table.shape))
        parts = lax.all_to_all(copies, "probe", 0, 0, tiled=True)
        parts, lower, upper = lax.optimization_barrier(
            (parts, probes[boxes - RIM :], probes[:RIM])
        )
        low = lax.ppermute(lower, "bfly", up)
        high = lax.ppermute(upper, "bfly", down)
        return pl.pallas_call(
            near_kernel,
            out_shape=pltpu.VMEM((boxes, cols, width), jnp.bfloat16),
            in_specs=[smem(), smem(), smem()] + [vmem()] * 5,
            out_specs=vmem(),
            scratch_shapes=[
                pltpu.VMEM((boxes + 2 * RIM, cols, width), jnp.bfloat16),
                pltpu.VMEM((boxes, cols, MAXB * width), jnp.bfloat16),
                pltpu.VMEM((MAXB * width, width), jnp.bfloat16),
            ],
            compiler_params=params(),
            cost_estimate=cost(rows, MAXB * width, width, 8 * rows * width),
            name="near_field",
        )(
            (lax.axis_index("bfly") * boxes)[None],
            near_cols,
            near_count,
            low,
            probes,
            high,
            near_scale,
            parts,
        )

    term = lax.cond(is_far, far_term, near_term, probes)
    other = lax.ppermute(term, "sec", [(0, 1), (1, 0)])
    term = lax.optimization_barrier(term)
    return term.astype(jnp.float32) + other.astype(jnp.float32)


def solution(mesh):
    return jax.shard_map(
        shards,
        mesh=mesh,
        in_specs=(
            P("bfly", "probe", None),
            P(),
            P(None, "bfly", None),
            P(None, "bfly"),
            P("bfly"),
            P("bfly", None),
            P("bfly", None, None),
            P(None, "probe", None),
        ),
        out_specs=P("bfly", "probe", None),
        check_vma=False,
    )
```

```python
import functools

import jax
import jax.numpy as jnp
from jax import lax
from jax.experimental import pallas as pl
from jax.experimental.pallas import tpu as pltpu
from jax.sharding import PartitionSpec as P

LOCAL = 4
MAXB = 6
RIM = 8
LOCAL_TILE = 2
CROSS_TILE = 8
VMEM_LIMIT = 40 * 1024 * 1024


def vmem():
    return pl.BlockSpec(memory_space=pltpu.VMEM)


def smem():
    return pl.BlockSpec(memory_space=pltpu.SMEM)


def hbm():
    return pl.BlockSpec(memory_space=pltpu.HBM)


def in_hbm(array):
    return pltpu.with_memory_space_constraint(array, pltpu.HBM)


def params():
    return pltpu.CompilerParams(vmem_limit_bytes=VMEM_LIMIT)


def cost(rows, depth, width, moved):
    return pl.CostEstimate(
        flops=2 * rows * depth * width, bytes_accessed=moved, transcendentals=0
    )


def local_kernel(
    orders_in, probes, mixers, gains_in, out, orders, gains, boxes_in, weights, pairs, sems, level_sems
):
    boxes, cols, width = out.shape
    fetches = [
        pltpu.make_async_copy(orders_in, orders, sems.at[0]),
        pltpu.make_async_copy(probes, boxes_in, sems.at[1]),
        pltpu.make_async_copy(gains_in, gains, sems.at[2]),
    ]
    loads = [
        pltpu.make_async_copy(mixers.at[level], weights.at[level], level_sems.at[level])
        for level in range(LOCAL)
    ]
    for copy in fetches + loads:
        copy.start()
    for copy in fetches:
        copy.wait()
    for level in range(LOCAL):
        source = boxes_in if level == 0 else out
        for box in range(boxes):
            block = source[orders[level, box]]
            pairs[box, :, :width] = block
            pairs[box ^ (1 << level), :, width:] = block
        loads[level].wait()
        for start in range(0, boxes, LOCAL_TILE):
            tile = slice(start, start + LOCAL_TILE)
            mixed = jnp.dot(
                pairs[tile].reshape(LOCAL_TILE * cols, 2 * width),
                weights[level],
                preferred_element_type=jnp.float32,
            ).reshape(LOCAL_TILE, cols, width)
            out[tile] = (mixed * gains[level, tile][:, None, :]).astype(out.dtype)


def cross_kernel(rows, mixers, out, pairs):
    count, depth, width = rows.shape
    levels = mixers.shape[0] - LOCAL
    for level in range(levels):
        source = rows if level == 0 else out
        for box in range(count):
            block = source[box]
            pairs[box, :, :width] = block
            pairs[box ^ (1 << level), :, width:] = block
        for start in range(0, count, CROSS_TILE):
            tile = slice(start, start + CROSS_TILE)
            mixed = jnp.dot(
                pairs[tile].reshape(CROSS_TILE * depth, 2 * width),
                mixers[LOCAL + level],
                preferred_element_type=jnp.float32,
            )
            out[tile] = mixed.reshape(CROSS_TILE, depth, width).astype(out.dtype)


def near_kernel(base, cols_ref, counts, low, own, high, scale, parts, out, extended, operand, table):
    boxes, cols, width = own.shape
    splits, slots, depth, _ = parts.shape
    for split in range(splits):
        for slot in range(slots):
            start = slot * width + split * depth
            table[start : start + depth] = parts[split, slot]
    extended[:RIM] = low[...]
    extended[RIM : RIM + boxes] = own[...]
    extended[RIM + boxes :] = high[...]
    first = base[0] - RIM
    for box in range(boxes):
        for slot in range(MAXB):
            block = extended[cols_ref[box, slot] - first].astype(jnp.float32)
            active = (slot < counts[box]).astype(jnp.float32)
            scaled = block * (scale[box, slot : slot + 1, :] * active)
            operand[box, :, slot * width : (slot + 1) * width] = scaled.astype(operand.dtype)
    out[...] = (
        jnp.dot(
            operand[...].reshape(boxes * cols, MAXB * width),
            table[...],
            preferred_element_type=jnp.float32,
        )
        .reshape(boxes, cols, width)
        .astype(out.dtype)
    )


def shards(probes, mixers, box_gains, box_orders, near_count, near_cols, near_scale, near_table):
    boxes, cols, width = probes.shape
    peers = lax.axis_size("bfly")
    levels = mixers.shape[0] - LOCAL
    rows = boxes * cols
    depth = rows // peers
    is_far = lax.axis_index("sec") == 1
    stacked = mixers.reshape(mixers.shape[0], 2 * width, width)

    def far_term(probes):
        current = pl.pallas_call(
            local_kernel,
            out_shape=jax.ShapeDtypeStruct((boxes, cols, width), jnp.bfloat16),
            in_specs=[hbm(), hbm(), hbm(), hbm()],
            out_specs=vmem(),
            scratch_shapes=[
                pltpu.SMEM((LOCAL, boxes), jnp.int32),
                pltpu.VMEM((LOCAL, boxes, width), jnp.float32),
                pltpu.VMEM((boxes, cols, width), jnp.bfloat16),
                pltpu.VMEM((LOCAL, 2 * width, width), jnp.bfloat16),
                pltpu.VMEM((boxes, cols, 2 * width), jnp.bfloat16),
                pltpu.SemaphoreType.DMA((3,)),
                pltpu.SemaphoreType.DMA((LOCAL,)),
            ],
            compiler_params=params(),
            cost_estimate=cost(LOCAL * rows, 2 * width, width, 4 * rows * width),
            name="local_levels",
        )(in_hbm(box_orders), in_hbm(probes), in_hbm(stacked), in_hbm(box_gains))
        current, later = lax.optimization_barrier((current, stacked))
        spread = lax.all_to_all(current.reshape(peers, depth, width), "bfly", 0, 0, tiled=True)
        crossed = pl.pallas_call(
            cross_kernel,
            out_shape=jax.ShapeDtypeStruct((peers, depth, width), jnp.bfloat16),
            in_specs=[vmem(), vmem()],
            out_specs=vmem(),
            scratch_shapes=[pltpu.VMEM((peers, depth, 2 * width), jnp.bfloat16)],
            compiler_params=params(),
            cost_estimate=cost(levels * rows, 2 * width, width, 4 * rows * width),
            name="cross_levels",
        )(spread, later)
        back = lax.all_to_all(crossed, "bfly", 0, 0, tiled=True)
        return back.reshape(boxes, cols, width)

    def near_term(probes):
        up = [(i, i + 1) for i in range(peers - 1)]
        down = [(i + 1, i) for i in range(peers - 1)]
        copies = jnp.broadcast_to(near_table, (lax.axis_size("probe"), *near_table.shape))
        parts = lax.all_to_all(copies, "probe", 0, 0, tiled=True)
        parts, upper = lax.optimization_barrier((parts, probes[:RIM]))
        low = lax.ppermute(probes[boxes - RIM :], "bfly", up)
        high = lax.ppermute(upper, "bfly", down)
        return pl.pallas_call(
            near_kernel,
            out_shape=pltpu.VMEM((boxes, cols, width), jnp.bfloat16),
            in_specs=[smem(), smem(), smem()] + [vmem()] * 5,
            out_specs=vmem(),
            scratch_shapes=[
                pltpu.VMEM((boxes + 2 * RIM, cols, width), jnp.bfloat16),
                pltpu.VMEM((boxes, cols, MAXB * width), jnp.bfloat16),
                pltpu.VMEM((MAXB * width, width), jnp.bfloat16),
            ],
            compiler_params=params(),
            cost_estimate=cost(rows, MAXB * width, width, 8 * rows * width),
            name="near_field",
        )(
            (lax.axis_index("bfly") * boxes)[None],
            near_cols,
            near_count,
            low,
            probes,
            high,
            near_scale,
            parts,
        )

    term = lax.cond(is_far, far_term, near_term, probes)
    other = lax.ppermute(term, "sec", [(0, 1), (1, 0)])
    term = lax.optimization_barrier(term)
    return term.astype(jnp.float32) + other.astype(jnp.float32)


def solution(mesh):
    return jax.shard_map(
        shards,
        mesh=mesh,
        in_specs=(
            P("bfly", "probe", None),
            P(),
            P(None, "bfly", None),
            P(None, "bfly"),
            P("bfly"),
            P("bfly", None),
            P("bfly", None, None),
            P(None, "probe", None),
        ),
        out_specs=P("bfly", "probe", None),
        check_vma=False,
    )
```

```python
import functools

import jax
import jax.numpy as jnp
from jax import lax
from jax.experimental import pallas as pl
from jax.experimental.pallas import tpu as pltpu
from jax.sharding import PartitionSpec as P

LOCAL = 4
MAXB = 6
RIM = 8
LOCAL_TILE = 2
CROSS_TILE = 8
SUM_TILE = 2
VMEM_LIMIT = 40 * 1024 * 1024


def vmem():
    return pl.BlockSpec(memory_space=pltpu.VMEM)


def smem():
    return pl.BlockSpec(memory_space=pltpu.SMEM)


def hbm():
    return pl.BlockSpec(memory_space=pltpu.HBM)


def in_hbm(array):
    return pltpu.with_memory_space_constraint(array, pltpu.HBM)


def params():
    return pltpu.CompilerParams(vmem_limit_bytes=VMEM_LIMIT)


def cost(rows, depth, width, moved):
    return pl.CostEstimate(
        flops=2 * rows * depth * width, bytes_accessed=moved, transcendentals=0
    )


def local_kernel(
    orders_in, probes, mixers, gains_in, out, orders, gains, boxes_in, weights, pairs, sems, level_sems
):
    boxes, cols, width = out.shape
    fetches = [
        pltpu.make_async_copy(orders_in, orders, sems.at[0]),
        pltpu.make_async_copy(probes, boxes_in, sems.at[1]),
        pltpu.make_async_copy(gains_in, gains, sems.at[2]),
    ]
    loads = [
        pltpu.make_async_copy(mixers.at[level], weights.at[level], level_sems.at[level])
        for level in range(LOCAL)
    ]
    for copy in fetches + loads:
        copy.start()
    for copy in fetches:
        copy.wait()
    for level in range(LOCAL):
        source = boxes_in if level == 0 else out
        for box in range(boxes):
            block = source[orders[level, box]]
            pairs[box, :, :width] = block
            pairs[box ^ (1 << level), :, width:] = block
        loads[level].wait()
        for start in range(0, boxes, LOCAL_TILE):
            tile = slice(start, start + LOCAL_TILE)
            mixed = jnp.dot(
                pairs[tile].reshape(LOCAL_TILE * cols, 2 * width),
                weights[level],
                preferred_element_type=jnp.float32,
            ).reshape(LOCAL_TILE, cols, width)
            out[tile] = (mixed * gains[level, tile][:, None, :]).astype(out.dtype)


def cross_kernel(rows, mixers, out, pairs):
    count, depth, width = rows.shape
    levels = mixers.shape[0] - LOCAL
    for level in range(levels):
        source = rows if level == 0 else out
        for box in range(count):
            block = source[box]
            pairs[box, :, :width] = block
            pairs[box ^ (1 << level), :, width:] = block
        for start in range(0, count, CROSS_TILE):
            tile = slice(start, start + CROSS_TILE)
            mixed = jnp.dot(
                pairs[tile].reshape(CROSS_TILE * depth, 2 * width),
                mixers[LOCAL + level],
                preferred_element_type=jnp.float32,
            )
            out[tile] = mixed.reshape(CROSS_TILE, depth, width).astype(out.dtype)


def near_kernel(base, cols_ref, counts, low, own, high, scale, parts, out, extended, operand, table):
    boxes, cols, width = own.shape
    splits, slots, depth, _ = parts.shape
    for split in range(splits):
        for slot in range(slots):
            start = slot * width + split * depth
            table[start : start + depth] = parts[split, slot]
    extended[:RIM] = low[...]
    extended[RIM : RIM + boxes] = own[...]
    extended[RIM + boxes :] = high[...]
    first = base[0] - RIM
    for box in range(boxes):
        for slot in range(MAXB):
            block = extended[cols_ref[box, slot] - first].astype(jnp.float32)
            active = (slot < counts[box]).astype(jnp.float32)
            scaled = block * (scale[box, slot : slot + 1, :] * active)
            operand[box, :, slot * width : (slot + 1) * width] = scaled.astype(operand.dtype)
    out[...] = (
        jnp.dot(
            operand[...].reshape(boxes * cols, MAXB * width),
            table[...],
            preferred_element_type=jnp.float32,
        )
        .reshape(boxes, cols, width)
        .astype(out.dtype)
    )


def sum_kernel(mine, other, out, total, sems):
    stores = []
    for start in range(0, out.shape[0], SUM_TILE):
        tile = pl.ds(start, SUM_TILE)
        total[tile] = mine[tile].astype(jnp.float32) + other[tile].astype(jnp.float32)
        store = pltpu.make_async_copy(total.at[tile], out.at[tile], sems.at[start // SUM_TILE])
        store.start()
        stores.append(store)
    for store in stores:
        store.wait()


def shards(probes, mixers, box_gains, box_orders, near_count, near_cols, near_scale, near_table):
    boxes, cols, width = probes.shape
    peers = lax.axis_size("bfly")
    levels = mixers.shape[0] - LOCAL
    rows = boxes * cols
    depth = rows // peers
    is_far = lax.axis_index("sec") == 1
    stacked = mixers.reshape(mixers.shape[0], 2 * width, width)

    def far_term(probes):
        current = pl.pallas_call(
            local_kernel,
            out_shape=jax.ShapeDtypeStruct((boxes, cols, width), jnp.bfloat16),
            in_specs=[hbm(), hbm(), hbm(), hbm()],
            out_specs=vmem(),
            scratch_shapes=[
                pltpu.SMEM((LOCAL, boxes), jnp.int32),
                pltpu.VMEM((LOCAL, boxes, width), jnp.float32),
                pltpu.VMEM((boxes, cols, width), jnp.bfloat16),
                pltpu.VMEM((LOCAL, 2 * width, width), jnp.bfloat16),
                pltpu.VMEM((boxes, cols, 2 * width), jnp.bfloat16),
                pltpu.SemaphoreType.DMA((3,)),
                pltpu.SemaphoreType.DMA((LOCAL,)),
            ],
            compiler_params=params(),
            cost_estimate=cost(LOCAL * rows, 2 * width, width, 4 * rows * width),
            name="local_levels",
        )(in_hbm(box_orders), in_hbm(probes), in_hbm(stacked), in_hbm(box_gains))
        current, later = lax.optimization_barrier((current, stacked))
        spread = lax.all_to_all(current.reshape(peers, depth, width), "bfly", 0, 0, tiled=True)
        crossed = pl.pallas_call(
            cross_kernel,
            out_shape=jax.ShapeDtypeStruct((peers, depth, width), jnp.bfloat16),
            in_specs=[vmem(), vmem()],
            out_specs=vmem(),
            scratch_shapes=[pltpu.VMEM((peers, depth, 2 * width), jnp.bfloat16)],
            compiler_params=params(),
            cost_estimate=cost(levels * rows, 2 * width, width, 4 * rows * width),
            name="cross_levels",
        )(spread, later)
        back = lax.all_to_all(crossed, "bfly", 0, 0, tiled=True)
        return back.reshape(boxes, cols, width)

    def near_term(probes):
        up = [(i, i + 1) for i in range(peers - 1)]
        down = [(i + 1, i) for i in range(peers - 1)]
        low = lax.ppermute(probes[boxes - RIM :], "bfly", up)
        high = lax.ppermute(probes[:RIM], "bfly", down)
        copies = jnp.broadcast_to(near_table, (lax.axis_size("probe"), *near_table.shape))
        parts = lax.all_to_all(copies, "probe", 0, 0, tiled=True)
        return pl.pallas_call(
            near_kernel,
            out_shape=pltpu.VMEM((boxes, cols, width), jnp.bfloat16),
            in_specs=[smem(), smem(), smem()] + [vmem()] * 5,
            out_specs=vmem(),
            scratch_shapes=[
                pltpu.VMEM((boxes + 2 * RIM, cols, width), jnp.bfloat16),
                pltpu.VMEM((boxes, cols, MAXB * width), jnp.bfloat16),
                pltpu.VMEM((MAXB * width, width), jnp.bfloat16),
            ],
            compiler_params=params(),
            cost_estimate=cost(rows, MAXB * width, width, 8 * rows * width),
            name="near_field",
        )(
            (lax.axis_index("bfly") * boxes)[None],
            near_cols,
            near_count,
            low,
            probes,
            high,
            near_scale,
            parts,
        )

    term = lax.cond(is_far, far_term, near_term, probes)
    other = lax.ppermute(term, "sec", [(0, 1), (1, 0)])
    term = lax.optimization_barrier(term)
    return pl.pallas_call(
        sum_kernel,
        out_shape=pltpu.HBM((boxes, cols, width), jnp.float32),
        in_specs=[vmem(), vmem()],
        out_specs=hbm(),
        scratch_shapes=[
            pltpu.VMEM((boxes, cols, width), jnp.float32),
            pltpu.SemaphoreType.DMA((boxes // SUM_TILE,)),
        ],
        compiler_params=params(),
        cost_estimate=cost(rows, 1, width, 8 * rows * width),
        name="response_sum",
    )(term, other)


def solution(mesh):
    return jax.shard_map(
        shards,
        mesh=mesh,
        in_specs=(
            P("bfly", "probe", None),
            P(),
            P(None, "bfly", None),
            P(None, "bfly"),
            P("bfly"),
            P("bfly", None),
            P("bfly", None, None),
            P(None, "probe", None),
        ),
        out_specs=P("bfly", "probe", None),
        check_vma=False,
    )
```
